32 devices in a mesh: groups: 2 (over x), expert: 16 (over z, y, core), node: 1.
Axes of the slice: x: 2, y: 2, z: 4, core: 2. Of those that a mesh axis runs over, the one named last changes fastest.
Arguments:
- tokens: bfloat16 [2048, 7168], P(('groups', 'expert'), 'node'), parts along dimension 0, may hold values from -6 to 6
- expert_ids: int32 [2048, 8], P(('groups', 'expert')), parts along dimension 0, may hold values from 0 to 15, all different within a row; in each aligned block of 64 rows (0 to 63, 64 to 127, ...) at most 40 rows name the same one
- gate_values: float32 [2048, 8], P(('groups', 'expert')), parts along dimension 0, may hold values from 0.05 to 1
- gate_weight: bfloat16 [16, 7168, 1024], P('expert', None, 'node'), may hold values from -1 to 1
- up_weight: bfloat16 [16, 7168, 1024], P('expert', None, 'node'), may hold values from -1 to 1
- down_weight: bfloat16 [16, 1024, 7168], P('expert', 'node'), may hold values from -1 to 1
- sketch: bfloat16 [7168, 512], P('node'), may hold values from -0.0625 to 0.0625
- subsets: int32 [64, 8], replicated, may hold values from 0 to 15, as said below
Outputs:
- combined: bfloat16 [2048, 512], P(('groups', 'expert'), 'node'), parts along dimension 0
- gram_matrix: float32 [32, 16], P('groups'), parts along dimension 0
- prune_error: float32 [128], P('groups'), parts along dimension 0
The draws below stay inside these ranges and needn't reach their ends.
There are 2 independent parts, one for each index of `groups`. The reference program is written for one: setup_inputs(seed, part) draws one part's arguments, and reference() takes and returns one part's arrays. A program takes and returns all parts, laid end to end along the dimension named above; an argument that names none is the same for every part. Nothing has to cross between parts.
Inputs may be any that keep to these rules, and one draw needn't show every extreme that they name: `expert_ids`: the ids of one token are distinct; among the 64 tokens of each aligned block no expert is chosen more than 40 times, a bound that some block reaches. `subsets`: each row names 8 different experts.
All inputs are finite; a program needn't handle non-finite values.
Results may differ from the reference program's by a relative error of at most 0.008.
Values may be sent and summed in bfloat16 or wider, within the bound.
A program may use at most 128 MiB of HBM per device.

```python
import math
import jax
import jax.numpy as jnp
import numpy as np
from jax import lax

D = 7168
TOPK = 8
FF = 1024
SK = 512
NSUB = 64
TOK_DEV = 64
EXPERTS = 16
TOKENS = 1024
CAP = 40
KEEP = 8
N_EXPERT = 16


def blend_weights(common, own_part, shared, fan_in):
    rest = math.sqrt(1.0 - shared * shared)
    mixed = (shared * common[None] + rest * own_part) / math.sqrt(fan_in)
    return mixed.astype(jnp.bfloat16)


def draw_gate_weight(key, part):
    key = jax.random.fold_in(key, 11)
    common_key, own_key = jax.random.split(key)
    common = jax.random.truncated_normal(common_key, -4.0, 4.0, (D, FF), jnp.float32)
    own_part = jax.random.truncated_normal(own_key, -4.0, 4.0, (EXPERTS, D, FF), jnp.float32)
    return blend_weights(common, own_part, 0.9, D)


def draw_up_weight(key, part):
    key = jax.random.fold_in(key, 13)
    common_key, own_key = jax.random.split(key)
    common = jax.random.truncated_normal(common_key, -4.0, 4.0, (D, FF), jnp.float32)
    own_part = jax.random.truncated_normal(own_key, -4.0, 4.0, (EXPERTS, D, FF), jnp.float32)
    return blend_weights(common, own_part, 0.9, D)


def draw_down_weight(key, part):
    key = jax.random.fold_in(key, 17)
    common_key, own_key = jax.random.split(key)
    common = jax.random.truncated_normal(common_key, -4.0, 4.0, (FF, D), jnp.float32)
    own_part = jax.random.truncated_normal(own_key, -4.0, 4.0, (EXPERTS, FF, D), jnp.float32)
    return blend_weights(common, own_part, 0.9, FF)


def draw_subsets(key, part):
    key = jax.random.fold_in(key, 7)
    row_keys = jax.random.split(key, NSUB)
    chosen = jax.vmap(lambda row_key: jax.random.permutation(row_key, EXPERTS)[:KEEP])(row_keys)
    return chosen.astype(jnp.int32)


def steps_of(stream_key, dims, cuts, smallest, largest):
    def one(position, blocks):
        heights = jax.random.uniform(jax.random.fold_in(jax.random.fold_in(stream_key, 6), position), (blocks,), jnp.float32, smallest / len(cuts), largest / len(cuts))
        return jnp.repeat(jnp.exp(heights), dims[position] // blocks).reshape((-1,) + (1,) * (len(dims) - position - 1))

    level = one(*cuts[0])
    for cut in cuts[1:]:
        level = level * one(*cut)
    return level


def shared_out(stream_key, own, number, rows, amount, top, reach, lean):
    sequence = jax.random.permutation(stream_key, amount)
    crowded, usual = load_shares(amount, rows * top, reach, lean, True), load_shares(amount, rows * top, reach, lean, False)
    places = jnp.arange(amount)

    def named(tallies, rotation):
        used = int((tallies > 0).sum())
        fixed = max(1, used // 4)
        moved = fixed + (places - fixed + rotation * (used - fixed)) % max(1, amount - fixed)
        return jnp.zeros((amount,), jnp.int32).at[sequence[jnp.where(places < fixed, places, moved)]].set(jnp.asarray(tallies, jnp.int32))

    tallies = jnp.where(number % 4 == 0, named(crowded, number // 4), named(usual, number - number // 4 - 1))
    mixed = jax.random.permutation(jax.random.fold_in(own, 3), amount)
    source_of, sink = mixed[0:amount // 2 * 2:2], mixed[1:amount // 2 * 2:2]
    margin = jnp.minimum(tallies[source_of] - 1, reach - tallies[sink]) // 2
    margin = jnp.where((source_of == sequence[0]) | (sink == sequence[0]) | (tallies[sink] == 0), 0, jnp.maximum(margin, 0))
    moved = jax.random.randint(jax.random.fold_in(own, 4), (amount // 2,), 0, 1 << 20) % (margin + 1)
    tallies = tallies.at[source_of].add(-moved).at[sink].add(moved)
    members = jnp.searchsorted(jnp.cumsum(tallies), jnp.arange(rows * top), side="right").astype(jnp.int32)
    grid = members.reshape(top, rows).T
    grid = grid[jax.random.permutation(jax.random.fold_in(own, 1), rows)]
    rotation = jax.random.randint(jax.random.fold_in(own, 2), (rows, 1), 0, top)
    return jnp.take_along_axis(grid, (jnp.arange(top)[None, :] + rotation) % top, axis=1)


def load_shares(count, total, most, slope, full):
    loads = [(1 << 20) // math.isqrt(grade ** slope) + 1 for grade in range(1, count + 1)]
    largest = most if full else min(most, max(-(-total // count), total * loads[0] // sum(loads)))
    least = 1 if total - largest >= count - 1 else 0
    given, spare = [largest] + [least] * (count - 1), total - largest - least * (count - 1)
    while spare > 0:
        free = [i for i in range(1, count) if given[i] < largest] or [i for i in range(1, count) if given[i] < most]
        pool, budget = sum([loads[i] for i in free]), spare
        for i in free:
            more = min(most - given[i], max(1, budget * loads[i] // pool), spare)
            given[i] = given[i] + more
            spare = spare - more
    return np.array(given)


def centred(stream_key, shape, width, reach, pieces=(), held_as=jnp.bfloat16):
    loudness = steps_of(stream_key, shape, pieces, -0.22, 0.18) if pieces else 1.0
    entries = jax.random.normal(stream_key, shape, jnp.float32) * width * loudness
    return jnp.minimum(jnp.maximum(entries, -reach), reach).astype(held_as)


def setup_inputs(seed: int = 0, part: int = 0) -> dict:
    key_of = jax.random.split(jax.random.key(seed), 9)
    part_splits = jax.random.split(jax.random.fold_in(key_of[8], part), 9)
    tokens = centred(part_splits[0], (TOKENS, D), 1.0, 6.0, ((0, 16),))
    expert_ids_keys = jax.random.split(jax.random.fold_in(part_splits[1], 1), TOKENS // TOK_DEV)
    expert_ids_turns = jax.random.permutation(jax.random.fold_in(part_splits[1], 3), TOKENS // TOK_DEV)
    expert_ids = jax.vmap(lambda own, number: shared_out(jax.random.fold_in(part_splits[1], 2), own, number, TOK_DEV, EXPERTS, TOPK, CAP, 1))(expert_ids_keys, expert_ids_turns).reshape((TOKENS, TOPK))
    gate_values = jnp.clip(0.05 + 0.95 * jax.random.uniform(part_splits[2], (TOKENS, TOPK), jnp.float32) ** steps_of(part_splits[2], (TOKENS, TOPK), ((0, 16),), -0.2, 0.2), 0.05, 1.0)
    gate_weight = draw_gate_weight(jax.random.fold_in(key_of[8], 71), part)
    up_weight = draw_up_weight(jax.random.fold_in(key_of[8], 71), part)
    down_weight = draw_down_weight(jax.random.fold_in(key_of[8], 71), part)
    sketch = centred(key_of[6], (D, SK), D ** -0.5, 0.0625)
    subsets = draw_subsets(jax.random.fold_in(key_of[8], 71), part)
    return {"tokens": tokens, "expert_ids": expert_ids, "gate_values": gate_values, "gate_weight": gate_weight, "up_weight": up_weight, "down_weight": down_weight, "sketch": sketch, "subsets": subsets}


def reference(tokens, expert_ids, gate_values, gate_weight, up_weight, down_weight, sketch, subsets):
    top_count = expert_ids.shape[1]
    expert_count = gate_weight.shape[0]
    capacity = min(TOK_DEV, TOK_DEV * TOPK * 5 // (4 * EXPERTS))
    most_rows = N_EXPERT * capacity
    flat_ids = expert_ids.reshape(-1).astype(jnp.int32)
    pair_count = flat_ids.shape[0]
    order = jnp.argsort(flat_ids, stable=True).astype(jnp.int32)
    labels = jnp.arange(expert_count, dtype=jnp.int32)
    counts = jnp.sum((flat_ids[:, None] == labels[None, :]).astype(jnp.int32), axis=0).astype(jnp.int32)
    offsets = (jnp.cumsum(counts) - counts).astype(jnp.int32)
    padded_order = jnp.concatenate([order, jnp.zeros((most_rows,), jnp.int32)])

    def one_expert(expert):
        begin_at = offsets[expert].astype(jnp.int32)
        pair_index = lax.dynamic_slice(padded_order, (begin_at,), (most_rows,))
        rows = jnp.take(tokens, pair_index // top_count, axis=0)
        sketched_down = jnp.dot(down_weight[expert], sketch, preferred_element_type=jnp.float32).astype(jnp.bfloat16)
        gate_part = jnp.dot(rows, gate_weight[expert], preferred_element_type=jnp.float32)
        up_part = jnp.dot(rows, up_weight[expert], preferred_element_type=jnp.float32)
        hidden = (jax.nn.silu(gate_part) * up_part).astype(jnp.bfloat16)
        result = jnp.dot(hidden, sketched_down, preferred_element_type=jnp.float32).astype(jnp.bfloat16)
        valid = jnp.arange(most_rows, dtype=jnp.int32) < counts[expert]
        target = jnp.where(valid, pair_index, pair_count).astype(jnp.int32)
        return result, target

    results, targets = lax.map(one_expert, labels)
    sketch_width = sketch.shape[1]
    pair_sketch = jnp.zeros((pair_count, sketch_width), jnp.bfloat16).at[targets.reshape(-1)].set(results.reshape(-1, sketch_width), mode="drop")
    pick_sketch = pair_sketch.reshape(-1, top_count, sketch_width).astype(jnp.float32)
    combined = jnp.einsum("tk,tkc->tc", gate_values, pick_sketch).astype(jnp.bfloat16)
    gated_sketch = gate_values[:, :, None] * pick_sketch
    pair_inner = jnp.einsum("tkc,tlc->tkl", gated_sketch, gated_sketch)
    routing = (expert_ids[:, :, None] == labels[None, None, :]).astype(jnp.float32)
    total_gram = jnp.einsum("tke,tkl,tlf->ef", routing, pair_inner, routing)
    gram_matrix = total_gram / (tokens.shape[0] * sketch_width)
    kept_mask = jnp.sum((subsets[:, :, None] == labels[None, None, :]).astype(jnp.float32), axis=1)
    pruned = 1.0 - kept_mask
    prune_error = jnp.einsum("se,ef,sf->s", pruned, gram_matrix, pruned) / jnp.sum(gram_matrix)
    return (combined, gram_matrix, prune_error)
```

```python
import jax
import jax.numpy as jnp
from jax import lax
from jax.experimental import pallas as pl
from jax.experimental.pallas import tpu as pltpu
from jax.sharding import PartitionSpec as P

STEPS = 14
LAG = 2
ROW_TILE = 256


def fused_kernel(
    tokens,
    ids,
    gates,
    gate_w,
    up_w,
    down_w,
    sketch,
    subsets,
    combined,
    gram_out,
    prune_out,
    xbuf,
    acc_gate,
    acc_up,
    acc_down,
    sd,
    wbuf,
    dbuf,
    sbuf,
    outbox,
    inbox,
    gated,
    gram_box,
    partial,
    recv_sem,
    up_sem,
    down_sem,
    side_sem,
    core_sem,
    w_sem,
    d_sem,
    back_send,
    back_recv,
    gram_send,
    gram_recv,
):
    me = lax.axis_index("expert")
    z, y, c = me // 4, (me // 2) % 2, me % 2
    above, below = me + 4, me - 4
    side = z * 4 + (1 - y) * 2 + c
    twin = z * 4 + y * 2 + (1 - c)
    rows, width = tokens.shape
    chunk = width // STEPS
    experts = 16

    def to(device):
        return {"expert": device}

    def weight_loads(k):
        slot = k % 2
        at = pl.ds(pl.multiple_of(k * chunk, chunk), chunk)
        return (
            pltpu.make_async_copy(gate_w.at[at, :], wbuf.at[slot, 0], w_sem.at[slot, 0]),
            pltpu.make_async_copy(up_w.at[at, :], wbuf.at[slot, 1], w_sem.at[slot, 1]),
        )

    def down_loads(k):
        slot = k % 2
        at = pl.ds(pl.multiple_of(k * chunk, chunk), chunk)
        return (
            pltpu.make_async_copy(down_w.at[:, at], dbuf.at[slot], d_sem.at[slot, 0]),
            pltpu.make_async_copy(sketch.at[at, :], sbuf.at[slot], d_sem.at[slot, 1]),
        )

    for load in down_loads(0) + weight_loads(0):
        load.start()

    barrier = pltpu.get_barrier_semaphore()
    for shift in range(1, experts):
        pl.semaphore_signal(
            barrier,
            inc=1,
            device_id=to((me + shift) % experts),
            device_id_type=pl.DeviceIdType.MESH,
        )
    for k in range(STEPS):
        xbuf[k, me] = tokens[:, k * chunk : (k + 1) * chunk]
    acc_gate[...] = jnp.zeros_like(acc_gate)
    acc_up[...] = jnp.zeros_like(acc_up)
    acc_down[...] = jnp.zeros_like(acc_down)
    pl.semaphore_wait(barrier, experts - 1)

    def send(k, block, sem, target):
        return pltpu.make_async_remote_copy(
            src_ref=xbuf.at[k, block],
            dst_ref=xbuf.at[k, block],
            send_sem=sem,
            recv_sem=recv_sem.at[k, block],
            device_id=to(target),
            device_id_type=pl.DeviceIdType.MESH,
        )

    def when_chunk(k, also=None):
        cond = (k >= 0) & (k < STEPS)
        return pl.when(cond if also is None else cond & also)

    def step(s, carry):
        for plane in range(4):
            dist = jnp.abs(z - plane)
            block = plane * 4 + y * 2 + c
            k = s - LAG * dist

            @when_chunk(k)
            def _():
                @pl.when(z != plane)
                def _():
                    send(k, block, up_sem.at[k, plane], twin).wait_recv()

                @pl.when((plane <= z) & (z < 3))
                def _():
                    send(k, block, up_sem.at[k, plane], above).start()

                @pl.when((plane >= z) & (z > 0))
                def _():
                    send(k, block, down_sem.at[k, plane], below).start()

                send(k, block, side_sem.at[k, plane], side).start()
                send(k, block, core_sem.at[k, plane], twin).start()

        for plane in range(4):
            dist = jnp.abs(z - plane)
            block = plane * 4 + (1 - y) * 2 + c
            k = s - LAG * (dist + 1)

            @when_chunk(k)
            def _():
                send(k, block, core_sem.at[k, 4 + plane], twin).wait_recv()
                send(k, block, core_sem.at[k, 4 + plane], twin).start()

        @pl.when(s < STEPS)
        def _():
            slot = s % 2

            @pl.when(s + 1 < STEPS)
            def _():
                for load in down_loads(s + 1):
                    load.start()

            for load in down_loads(s):
                load.wait()

            @pl.loop(0, down_w.shape[0] // ROW_TILE)
            def _(r):
                at = pl.ds(pl.multiple_of(r * ROW_TILE, ROW_TILE), ROW_TILE)
                acc_down[at, :] += jnp.dot(
                    dbuf[slot, at, :], sbuf[slot], preferred_element_type=jnp.float32
                )

        k = s - 5 * LAG

        @when_chunk(k)
        def _():
            slot = k % 2

            @pl.when(k + 1 < STEPS)
            def _():
                for load in weight_loads(k + 1):
                    load.start()

            for plane in range(4):
                for col in range(2):
                    block = plane * 4 + col * 2 + (1 - c)
                    send(k, block, up_sem.at[k, plane], twin).wait_recv()
            for load in weight_loads(k):
                load.wait()

            @pl.loop(0, experts * rows // ROW_TILE)
            def _(r):
                per = ROW_TILE // rows
                at = pl.ds(pl.multiple_of(r * ROW_TILE, ROW_TILE), ROW_TILE)
                x = xbuf[k, pl.ds(r * per, per)].reshape(ROW_TILE, chunk)
                acc_gate[at, :] += jnp.dot(x, wbuf[slot, 0], preferred_element_type=jnp.float32)
                acc_up[at, :] += jnp.dot(x, wbuf[slot, 1], preferred_element_type=jnp.float32)

        return carry

    lax.fori_loop(0, STEPS + 5 * LAG, step, 0)

    sd[...] = acc_down[...].astype(jnp.bfloat16)

    def back(block):
        return pltpu.make_async_remote_copy(
            src_ref=outbox.at[block],
            dst_ref=inbox.at[me],
            send_sem=back_send.at[block],
            recv_sem=back_recv.at[me],
            device_id=to(block),
            device_id_type=pl.DeviceIdType.MESH,
        )

    def finish(i, carry):
        plane = (z + 1 + i) % 4
        at = pl.ds(pl.multiple_of(plane * 4 * rows, 4 * rows), 4 * rows)
        g = acc_gate[at, :]
        hidden = (g / (1.0 + jnp.exp(-g)) * acc_up[at, :]).astype(jnp.bfloat16)
        result = jnp.dot(hidden, sd[...], preferred_element_type=jnp.float32).astype(jnp.bfloat16)
        outbox[pl.ds(plane * 4, 4)] = result.reshape(4, rows, -1)
        for j in range(4):
            block = plane * 4 + j

            @pl.when(block != me)
            def _():
                back(block).start()

        return carry

    lax.fori_loop(0, 4, finish, 0)
    inbox[me] = outbox[me]

    def arrived(e):
        return pltpu.make_async_remote_copy(
            src_ref=outbox.at[e],
            dst_ref=inbox.at[e],
            send_sem=back_send.at[e],
            recv_sem=back_recv.at[e],
            device_id=to(twin),
            device_id_type=pl.DeviceIdType.MESH,
        )

    total = jnp.zeros(combined.shape, jnp.float32)
    for e in range(experts):

        @pl.when(me != e)
        def _():
            arrived(e).wait_recv()

        gate = jnp.sum(jnp.where(ids[...] == e, gates[...], 0.0), axis=1, keepdims=True)
        part = gate * inbox[e].astype(jnp.float32)
        total = total + part
        gated[e * rows : (e + 1) * rows, :] = part.astype(jnp.bfloat16)
    combined[...] = total.astype(combined.dtype)

    flat = experts * rows
    tile = 4 * rows
    row_tok = lax.broadcasted_iota(jnp.int32, (tile, flat), 0) % rows
    col_tok = lax.broadcasted_iota(jnp.int32, (tile, flat), 1) % rows
    same = row_tok == col_tok
    for r in range(4):
        pair = lax.dot_general(
            gated[r * tile : (r + 1) * tile, :],
            gated[...],
            (((1,), (1,)), ((), ())),
            preferred_element_type=jnp.float32,
        )
        pair = jnp.where(same, pair, 0.0).reshape(4, rows, flat)
        partial[r * 4 : (r + 1) * 4, :] = jnp.sum(pair, axis=1)
    owner = lax.broadcasted_iota(jnp.int32, (flat, experts), 0) // rows
    label = lax.broadcasted_iota(jnp.int32, (flat, experts), 1)
    local = jnp.dot(
        partial[...],
        (owner == label).astype(jnp.float32),
        preferred_element_type=jnp.float32,
        precision=lax.Precision.HIGHEST,
    )
    gram_box[me] = local

    def share(shift):
        other = (me + shift) % experts
        return pltpu.make_async_remote_copy(
            src_ref=gram_box.at[me],
            dst_ref=gram_box.at[me],
            send_sem=gram_send.at[shift],
            recv_sem=gram_recv.at[me],
            device_id=to(other),
            device_id_type=pl.DeviceIdType.MESH,
        )

    def shared(e):
        return pltpu.make_async_remote_copy(
            src_ref=gram_box.at[e],
            dst_ref=gram_box.at[e],
            send_sem=gram_send.at[0],
            recv_sem=gram_recv.at[e],
            device_id=to(twin),
            device_id_type=pl.DeviceIdType.MESH,
        )

    for shift in range(1, experts):
        share(shift).start()
    names = subsets[...]
    columns = lax.broadcasted_iota(jnp.int32, (names.shape[0], experts), 1)
    kept = jnp.zeros((names.shape[0], experts), jnp.float32)
    for j in range(names.shape[1]):
        kept = kept + jnp.where(names[:, j : j + 1] == columns, 1.0, 0.0)
    pruned = 1.0 - kept

    def collect(k, carry):
        for plane in range(4):
            block = plane * 4 + y * 2 + c
            across = plane * 4 + (1 - y) * 2 + c

            @pl.when((plane <= z) & (z < 3))
            def _():
                send(k, block, up_sem.at[k, plane], above).wait_send()

            @pl.when((plane >= z) & (z > 0))
            def _():
                send(k, block, down_sem.at[k, plane], below).wait_send()

            send(k, block, side_sem.at[k, plane], side).wait_send()
            send(k, block, core_sem.at[k, plane], twin).wait_send()
            send(k, across, core_sem.at[k, 4 + plane], twin).wait_send()
        return carry

    lax.fori_loop(0, STEPS, collect, 0)
    for e in range(experts):

        @pl.when(me != e)
        def _():
            arrived(e).wait_send()

    for e in range(experts):

        @pl.when(me != e)
        def _():
            shared(e).wait_recv()

    gram = jnp.sum(gram_box[...], axis=0) / (rows * experts * sketch.shape[1])
    gram_out[...] = gram
    weighed = jnp.dot(
        pruned, gram, preferred_element_type=jnp.float32, precision=lax.Precision.HIGHEST
    )
    prune_out[...] = jnp.sum(weighed * pruned, axis=1, keepdims=True) / jnp.sum(gram)
    for shift in range(1, experts):
        share(shift).wait_send()


def fused(tokens, expert_ids, gate_values, gate_weight, up_weight, down_weight, sketch, subsets):
    rows, width = tokens.shape
    experts = 16
    chunk = width // STEPS
    hidden_width = gate_weight.shape[2]
    sketch_width = sketch.shape[1]
    bf16, f32 = jnp.bfloat16, jnp.float32
    dma = pltpu.SemaphoreType.DMA
    vmem = pl.BlockSpec(memory_space=pltpu.VMEM)
    hbm = pl.BlockSpec(memory_space=pl.ANY)
    combined, gram, prune = pl.pallas_call(
        fused_kernel,
        out_shape=(
            jax.ShapeDtypeStruct((rows, sketch_width), bf16),
            jax.ShapeDtypeStruct((experts, experts), f32),
            jax.ShapeDtypeStruct((subsets.shape[0], 1), f32),
        ),
        in_specs=[vmem, vmem, vmem, hbm, hbm, hbm, hbm, vmem],
        out_specs=(vmem, vmem, vmem),
        scratch_shapes=[
            pltpu.VMEM((STEPS, experts, rows, chunk), bf16),
            pltpu.VMEM((experts * rows, hidden_width), f32),
            pltpu.VMEM((experts * rows, hidden_width), f32),
            pltpu.VMEM((hidden_width, sketch_width), f32),
            pltpu.VMEM((hidden_width, sketch_width), bf16),
            pltpu.VMEM((2, 2, chunk, hidden_width), bf16),
            pltpu.VMEM((2, hidden_width, chunk), bf16),
            pltpu.VMEM((2, chunk, sketch_width), bf16),
            pltpu.VMEM((experts, rows, sketch_width), bf16),
            pltpu.VMEM((experts, rows, sketch_width), bf16),
            pltpu.VMEM((experts * rows, sketch_width), bf16),
            pltpu.VMEM((experts, experts, experts), f32),
            pltpu.VMEM((experts, experts * rows), f32),
            dma((STEPS, experts)),
            dma((STEPS, 4)),
            dma((STEPS, 4)),
            dma((STEPS, 4)),
            dma((STEPS, 8)),
            dma((2, 2)),
            dma((2, 2)),
            dma((experts,)),
            dma((experts,)),
            dma((experts,)),
            dma((experts,)),
        ],
        compiler_params=pltpu.CompilerParams(
            collective_id=0, has_side_effects=True, vmem_limit_bytes=58 * 1024 * 1024
        ),
    )(
        tokens,
        expert_ids,
        gate_values,
        gate_weight.reshape(gate_weight.shape[1:]),
        up_weight.reshape(up_weight.shape[1:]),
        down_weight.reshape(down_weight.shape[1:]),
        sketch,
        subsets,
    )
    return combined, gram, prune.reshape(-1)


def shards(tokens, expert_ids, gate_values, gate_weight, up_weight, down_weight, sketch, subsets):
    experts = lax.axis_size("expert")
    tok_rows = expert_ids.shape[0]
    top_count = expert_ids.shape[1]
    capacity = min(tok_rows, tok_rows * top_count * 5 // (4 * experts))
    flat_ids = expert_ids.reshape(-1)
    pick_count = flat_ids.shape[0]
    labels = jnp.arange(experts, dtype=jnp.int32)
    member = (flat_ids[:, None] == labels[None, :]).astype(jnp.int32)
    position = jnp.sum((jnp.cumsum(member, axis=0) - 1) * member, axis=1)
    slot_index = flat_ids * capacity + position
    source_row = jnp.arange(pick_count, dtype=jnp.int32) // top_count
    row_table = jnp.zeros((experts * capacity,), jnp.int32).at[slot_index].set(source_row)
    filled = jnp.zeros((experts * capacity,), jnp.bfloat16).at[slot_index].set(1.0)
    whole_rows = lax.all_gather(tokens, "node", axis=1, tiled=True)
    picked = jnp.take(whole_rows, row_table, axis=0) * filled[:, None]
    arrived = lax.all_to_all(
        picked.reshape(experts, capacity, whole_rows.shape[1]),
        "expert",
        split_axis=0,
        concat_axis=0,
        tiled=True,
    )
    model_width = arrived.shape[2]
    slot_rows = arrived.reshape(-1, model_width)
    down_local = down_weight[0]
    sketch_width = sketch.shape[1]
    sketched_down = jnp.dot(
        down_local,
        lax.all_gather(sketch, "node", axis=0, tiled=True),
        preferred_element_type=jnp.float32,
    ).astype(jnp.bfloat16)
    gate_part = jnp.dot(slot_rows, gate_weight[0], preferred_element_type=jnp.float32)
    up_part = jnp.dot(slot_rows, up_weight[0], preferred_element_type=jnp.float32)
    hidden = (jax.nn.silu(gate_part) * up_part).astype(jnp.bfloat16)
    partial_sketch = jnp.dot(hidden, sketched_down, preferred_element_type=jnp.float32)
    returned = lax.all_to_all(
        partial_sketch.reshape(experts, capacity, sketch_width),
        "expert",
        split_axis=0,
        concat_axis=0,
        tiled=True,
    )
    slot_sketch = lax.psum_scatter(returned, "node", scatter_dimension=2, tiled=True).astype(
        jnp.bfloat16
    )
    half_width = slot_sketch.shape[2]
    pick_sketch = jnp.take(slot_sketch.reshape(-1, half_width), slot_index, axis=0)
    pick_sketch = pick_sketch.reshape(tok_rows, top_count, half_width).astype(jnp.float32)
    combined = jnp.einsum("tk,tkc->tc", gate_values, pick_sketch).astype(jnp.bfloat16)
    gated_sketch = gate_values[:, :, None] * pick_sketch
    pair_inner = jnp.einsum("tkc,tlc->tkl", gated_sketch, gated_sketch)
    routing = (expert_ids[:, :, None] == labels[None, None, :]).astype(jnp.float32)
    local_gram = jnp.einsum("tke,tkl,tlf->ef", routing, pair_inner, routing)
    total_gram = lax.psum(local_gram, ("expert", "node"))
    gram_matrix = total_gram / (tok_rows * experts * sketch_width)
    kept_mask = jnp.sum((subsets[:, :, None] == labels[None, None, :]).astype(jnp.float32), axis=1)
    pruned = 1.0 - kept_mask
    prune_error = jnp.einsum("se,ef,sf->s", pruned, gram_matrix, pruned) / jnp.sum(gram_matrix)
    return (combined, gram_matrix, prune_error)


def solution(mesh):
    in_specs = (
        P(("groups", "expert"), "node"),
        P(("groups", "expert"), None),
        P(("groups", "expert"), None),
        P("expert", None, "node"),
        P("expert", None, "node"),
        P("expert", "node", None),
        P("node", None),
        P(),
    )
    out_specs = (P(("groups", "expert"), "node"), P("groups", None), P("groups"))
    plain = mesh.shape["node"] == 1 and mesh.shape["expert"] == 16
    return jax.shard_map(fused if plain else shards, mesh=mesh, in_specs=in_specs, out_specs=out_specs, check_vma=False)
```

```python
import jax
import jax.numpy as jnp
from jax import lax
from jax.experimental import pallas as pl
from jax.experimental.pallas import tpu as pltpu
from jax.sharding import PartitionSpec as P

STEPS = 14
LAG = 1
BOTH = 7
ROW_TILE = 256


def fused_kernel(
    tokens,
    ids,
    gates,
    gate_w,
    up_w,
    down_w,
    sketch,
    subsets,
    combined,
    gram_out,
    prune_out,
    xbuf,
    acc_gate,
    acc_up,
    acc_down,
    sd,
    wbuf,
    dbuf,
    sbuf,
    outbox,
    inbox,
    gated,
    gram_box,
    partial,
    recv_sem,
    up_sem,
    down_sem,
    side_sem,
    core_sem,
    w_sem,
    d_sem,
    slots_out,
    slots_in,
    cross_up,
    cross_down,
    slot_send,
    slot_recv,
    back_send,
    back_recv,
    gram_send,
    gram_recv,
):
    me = lax.axis_index("expert")
    z, y, c = me // 4, (me // 2) % 2, me % 2
    above, below = me + 4, me - 4
    side = z * 4 + (1 - y) * 2 + c
    twin = z * 4 + y * 2 + (1 - c)
    rows, width = tokens.shape
    chunk = width // STEPS
    experts = 16

    def to(device):
        return {"expert": device}

    def weight_loads(k):
        slot = k % 2
        at = pl.ds(pl.multiple_of(k * chunk, chunk), chunk)
        return (
            pltpu.make_async_copy(gate_w.at[at, :], wbuf.at[slot, 0], w_sem.at[slot, 0]),
            pltpu.make_async_copy(up_w.at[at, :], wbuf.at[slot, 1], w_sem.at[slot, 1]),
        )

    def down_loads(k):
        slot = k % 2
        at = pl.ds(pl.multiple_of(k * chunk, chunk), chunk)
        return (
            pltpu.make_async_copy(down_w.at[:, at], dbuf.at[slot], d_sem.at[slot, 0]),
            pltpu.make_async_copy(sketch.at[at, :], sbuf.at[slot], d_sem.at[slot, 1]),
        )

    for load in down_loads(0) + weight_loads(0):
        load.start()

    barrier = pltpu.get_barrier_semaphore()
    for shift in range(1, experts):
        pl.semaphore_signal(
            barrier,
            inc=1,
            device_id=to((me + shift) % experts),
            device_id_type=pl.DeviceIdType.MESH,
        )
    for k in range(STEPS):
        xbuf[k, me] = tokens[:, k * chunk : (k + 1) * chunk]
    acc_gate[...] = jnp.zeros_like(acc_gate)
    acc_up[...] = jnp.zeros_like(acc_up)
    acc_down[...] = jnp.zeros_like(acc_down)

    capacity = outbox.shape[1] // 2
    lanes = lax.broadcasted_iota(jnp.int32, (rows, experts), 1)
    member = jnp.zeros((rows, experts), jnp.float32)
    for j in range(ids.shape[1]):
        member = member + jnp.where(ids[:, j : j + 1] == lanes, 1.0, 0.0)
    member = member.astype(jnp.bfloat16)
    first = lax.broadcasted_iota(jnp.int32, (rows, 2 * rows), 0)
    second = lax.broadcasted_iota(jnp.int32, (rows, 2 * rows), 1) % rows

    def turned(mask):
        return lax.dot_general(
            member,
            jnp.where(mask, 1.0, 0.0).astype(jnp.bfloat16),
            (((0,), (0,)), ((), ())),
            preferred_element_type=jnp.float32,
        )

    slots = jnp.where(turned(first == second) > 0.5, turned(first < second), -1.0)
    for e in range(experts):
        slots_out[e] = jnp.broadcast_to(slots[e : e + 1, :], (8, 2 * rows))
    slots_in[me] = slots_out[me]

    def picker(row):
        shape = (2 * capacity, 2 * rows)
        place = lax.broadcasted_iota(jnp.int32, shape, 0)
        half = lax.broadcasted_iota(jnp.int32, shape, 1) >= rows
        late = place >= capacity
        wanted = jnp.where(late, place - capacity, place).astype(jnp.float32)
        wanted = jnp.where(late == half, wanted, -2.0)
        return jnp.where(row == wanted, 1.0, 0.0).astype(jnp.bfloat16)

    pl.semaphore_wait(barrier, experts - 1)

    def send(k, block, sem, target):
        return pltpu.make_async_remote_copy(
            src_ref=xbuf.at[k, block],
            dst_ref=xbuf.at[k, block],
            send_sem=sem,
            recv_sem=recv_sem.at[k, block],
            device_id=to(target),
            device_id_type=pl.DeviceIdType.MESH,
        )

    def slot_copy(block):
        return pltpu.make_async_remote_copy(
            src_ref=slots_out.at[block],
            dst_ref=slots_in.at[me],
            send_sem=slot_send.at[block],
            recv_sem=slot_recv.at[me],
            device_id=to(block),
            device_id_type=pl.DeviceIdType.MESH,
        )

    def slot_arrived(e):
        return pltpu.make_async_remote_copy(
            src_ref=slots_out.at[e],
            dst_ref=slots_in.at[e],
            send_sem=slot_send.at[e],
            recv_sem=slot_recv.at[e],
            device_id=to(twin),
            device_id_type=pl.DeviceIdType.MESH,
        )

    for e in range(experts):

        @pl.when(me != e)
        def _():
            slot_copy(e).start()

    def when_chunk(k, also=None):
        cond = (k >= 0) & (k < STEPS)
        return pl.when(cond if also is None else cond & also)

    def step(s, carry):
        for plane in range(4):
            dist = jnp.abs(z - plane)
            block = plane * 4 + y * 2 + c
            k = s - LAG * dist

            @when_chunk(k)
            def _():
                @pl.when(z != plane)
                def _():
                    send(k, block, up_sem.at[k, plane], twin).wait_recv()

                @pl.when((plane <= z) & (z < 3))
                def _():
                    send(k, block, up_sem.at[k, plane], above).start()

                @pl.when((plane >= z) & (z > 0))
                def _():
                    send(k, block, down_sem.at[k, plane], below).start()

                @pl.when((z == plane) | (k % BOTH != 0))
                def _():
                    send(k, block, side_sem.at[k, plane], side).start()

                send(k, block, core_sem.at[k, plane], twin).start()

        for plane in range(4):
            dist = jnp.abs(z - plane)
            block = plane * 4 + (1 - y) * 2 + c
            k = s - LAG * (dist + 1)

            @when_chunk(k)
            def _():
                send(k, block, core_sem.at[k, 4 + plane], twin).wait_recv()

                @pl.when((plane <= z) & (z < 3) & (k % BOTH == 0))
                def _():
                    send(k, block, cross_up.at[k, plane], above).start()

                @pl.when((plane >= z) & (z > 0) & (k % BOTH == 0))
                def _():
                    send(k, block, cross_down.at[k, plane], below).start()

                send(k, block, core_sem.at[k, 4 + plane], twin).start()

        @pl.when(s < STEPS)
        def _():
            slot = s % 2

            @pl.when(s + 1 < STEPS)
            def _():
                for load in down_loads(s + 1):
                    load.start()

            for load in down_loads(s):
                load.wait()

            @pl.loop(0, down_w.shape[0] // ROW_TILE)
            def _(r):
                at = pl.ds(pl.multiple_of(r * ROW_TILE, ROW_TILE), ROW_TILE)
                acc_down[at, :] += jnp.dot(
                    dbuf[slot, at, :], sbuf[slot], preferred_element_type=jnp.float32
                )

        k = s - 5 * LAG

        @when_chunk(k)
        def _():
            slot = k % 2

            @pl.when(k + 1 < STEPS)
            def _():
                for load in weight_loads(k + 1):
                    load.start()

            for plane in range(4):
                for col in range(2):
                    block = plane * 4 + col * 2 + (1 - c)
                    send(k, block, up_sem.at[k, plane], twin).wait_recv()
            for load in weight_loads(k):
                load.wait()

            @pl.loop(0, experts * rows // ROW_TILE)
            def _(r):
                per = ROW_TILE // rows
                at = pl.ds(pl.multiple_of(r * ROW_TILE, ROW_TILE), ROW_TILE)
                x = xbuf[k, pl.ds(r * per, per)].reshape(ROW_TILE, chunk)
                acc_gate[at, :] += jnp.dot(x, wbuf[slot, 0], preferred_element_type=jnp.float32)
                acc_up[at, :] += jnp.dot(x, wbuf[slot, 1], preferred_element_type=jnp.float32)

        return carry

    lax.fori_loop(0, STEPS + 5 * LAG, step, 0)

    sd[...] = acc_down[...].astype(jnp.bfloat16)

    for e in range(experts):

        @pl.when(me != e)
        def _():
            slot_arrived(e).wait_recv()

    half_width = sd.shape[1] // 2

    def back(block):
        return pltpu.make_async_remote_copy(
            src_ref=outbox.at[block],
            dst_ref=inbox.at[me],
            send_sem=back_send.at[block],
            recv_sem=back_recv.at[me],
            device_id=to(block),
            device_id_type=pl.DeviceIdType.MESH,
        )

    def finish(i, carry):
        plane = (z + 1 + i) % 4
        at = pl.ds(pl.multiple_of(plane * 4 * rows, 4 * rows), 4 * rows)
        g = acc_gate[at, :]
        hidden = (g / (1.0 + jnp.exp(-g)) * acc_up[at, :]).astype(jnp.bfloat16)
        result = jnp.dot(hidden, sd[...], preferred_element_type=jnp.float32).astype(jnp.bfloat16)
        for j in range(4):
            block = plane * 4 + j
            mine = result[j * rows : (j + 1) * rows]
            mine = jnp.concatenate([mine[:, :half_width], mine[:, half_width:]], axis=0)
            outbox[block] = jnp.dot(
                picker(slots_in[block][0:1, :]), mine, preferred_element_type=jnp.float32
            ).astype(jnp.bfloat16)

            @pl.when(block != me)
            def _():
                back(block).start()

        return carry

    lax.fori_loop(0, 4, finish, 0)
    inbox[me] = outbox[me]

    def arrived(e):
        return pltpu.make_async_remote_copy(
            src_ref=outbox.at[e],
            dst_ref=inbox.at[e],
            send_sem=back_send.at[e],
            recv_sem=back_recv.at[e],
            device_id=to(twin),
            device_id_type=pl.DeviceIdType.MESH,
        )

    total = jnp.zeros(combined.shape, jnp.float32)
    for e in range(experts):

        @pl.when(me != e)
        def _():
            arrived(e).wait_recv()

        gate = jnp.sum(jnp.where(ids[...] == e, gates[...], 0.0), axis=1, keepdims=True)
        spread = lax.dot_general(
            picker(slots_out[e][0:1, :]),
            inbox[e],
            (((0,), (0,)), ((), ())),
            preferred_element_type=jnp.float32,
        )
        part = gate * jnp.concatenate([spread[:rows], spread[rows:]], axis=1)
        total = total + part
        gated[e * rows : (e + 1) * rows, :] = part.astype(jnp.bfloat16)
    combined[...] = total.astype(combined.dtype)

    flat = experts * rows
    tile = 4 * rows
    row_tok = lax.broadcasted_iota(jnp.int32, (tile, flat), 0) % rows
    col_tok = lax.broadcasted_iota(jnp.int32, (tile, flat), 1) % rows
    same = row_tok == col_tok
    for r in range(4):
        pair = lax.dot_general(
            gated[r * tile : (r + 1) * tile, :],
            gated[...],
            (((1,), (1,)), ((), ())),
            preferred_element_type=jnp.float32,
        )
        pair = jnp.where(same, pair, 0.0).reshape(4, rows, flat)
        partial[r * 4 : (r + 1) * 4, :] = jnp.sum(pair, axis=1)
    owner = lax.broadcasted_iota(jnp.int32, (flat, experts), 0) // rows
    label = lax.broadcasted_iota(jnp.int32, (flat, experts), 1)
    local = jnp.dot(
        partial[...],
        (owner == label).astype(jnp.float32),
        preferred_element_type=jnp.float32,
        precision=lax.Precision.HIGHEST,
    )
    gram_box[me] = local

    def share(shift):
        other = (me + shift) % experts
        return pltpu.make_async_remote_copy(
            src_ref=gram_box.at[me],
            dst_ref=gram_box.at[me],
            send_sem=gram_send.at[shift],
            recv_sem=gram_recv.at[me],
            device_id=to(other),
            device_id_type=pl.DeviceIdType.MESH,
        )

    def shared(e):
        return pltpu.make_async_remote_copy(
            src_ref=gram_box.at[e],
            dst_ref=gram_box.at[e],
            send_sem=gram_send.at[0],
            recv_sem=gram_recv.at[e],
            device_id=to(twin),
            device_id_type=pl.DeviceIdType.MESH,
        )

    for shift in range(1, experts):
        share(shift).start()
    names = subsets[...]
    columns = lax.broadcasted_iota(jnp.int32, (names.shape[0], experts), 1)
    kept = jnp.zeros((names.shape[0], experts), jnp.float32)
    for j in range(names.shape[1]):
        kept = kept + jnp.where(names[:, j : j + 1] == columns, 1.0, 0.0)
    pruned = 1.0 - kept

    def collect(k, carry):
        for plane in range(4):
            block = plane * 4 + y * 2 + c
            across = plane * 4 + (1 - y) * 2 + c

            @pl.when((plane <= z) & (z < 3))
            def _():
                send(k, block, up_sem.at[k, plane], above).wait_send()

            @pl.when((plane >= z) & (z > 0))
            def _():
                send(k, block, down_sem.at[k, plane], below).wait_send()

            @pl.when((z == plane) | (k % BOTH != 0))
            def _():
                send(k, block, side_sem.at[k, plane], side).wait_send()

            @pl.when((plane <= z) & (z < 3) & (k % BOTH == 0))
            def _():
                send(k, across, cross_up.at[k, plane], above).wait_send()

            @pl.when((plane >= z) & (z > 0) & (k % BOTH == 0))
            def _():
                send(k, across, cross_down.at[k, plane], below).wait_send()

            send(k, block, core_sem.at[k, plane], twin).wait_send()
            send(k, across, core_sem.at[k, 4 + plane], twin).wait_send()
        return carry

    lax.fori_loop(0, STEPS, collect, 0)
    for e in range(experts):

        @pl.when(me != e)
        def _():
            arrived(e).wait_send()
            slot_arrived(e).wait_send()

    for e in range(experts):

        @pl.when(me != e)
        def _():
            shared(e).wait_recv()

    gram = jnp.sum(gram_box[...], axis=0) / (rows * experts * sketch.shape[1])
    gram_out[...] = gram
    weighed = jnp.dot(
        pruned, gram, preferred_element_type=jnp.float32, precision=lax.Precision.HIGHEST
    )
    prune_out[...] = jnp.sum(weighed * pruned, axis=1, keepdims=True) / jnp.sum(gram)
    for shift in range(1, experts):
        share(shift).wait_send()


def fused(tokens, expert_ids, gate_values, gate_weight, up_weight, down_weight, sketch, subsets):
    rows, width = tokens.shape
    experts = 16
    chunk = width // STEPS
    capacity = min(rows, rows * expert_ids.shape[1] * 5 // (4 * experts))
    hidden_width = gate_weight.shape[2]
    sketch_width = sketch.shape[1]
    bf16, f32 = jnp.bfloat16, jnp.float32
    dma = pltpu.SemaphoreType.DMA
    vmem = pl.BlockSpec(memory_space=pltpu.VMEM)
    hbm = pl.BlockSpec(memory_space=pl.ANY)
    combined, gram, prune = pl.pallas_call(
        fused_kernel,
        out_shape=(
            jax.ShapeDtypeStruct((rows, sketch_width), bf16),
            jax.ShapeDtypeStruct((experts, experts), f32),
            jax.ShapeDtypeStruct((subsets.shape[0], 1), f32),
        ),
        in_specs=[vmem, vmem, vmem, hbm, hbm, hbm, hbm, vmem],
        out_specs=(vmem, vmem, vmem),
        scratch_shapes=[
            pltpu.VMEM((STEPS, experts, rows, chunk), bf16),
            pltpu.VMEM((experts * rows, hidden_width), f32),
            pltpu.VMEM((experts * rows, hidden_width), f32),
            pltpu.VMEM((hidden_width, sketch_width), f32),
            pltpu.VMEM((hidden_width, sketch_width), bf16),
            pltpu.VMEM((2, 2, chunk, hidden_width), bf16),
            pltpu.VMEM((2, hidden_width, chunk), bf16),
            pltpu.VMEM((2, chunk, sketch_width), bf16),
            pltpu.VMEM((experts, 2 * capacity, sketch_width // 2), bf16),
            pltpu.VMEM((experts, 2 * capacity, sketch_width // 2), bf16),
            pltpu.VMEM((experts * rows, sketch_width), bf16),
            pltpu.VMEM((experts, experts, experts), f32),
            pltpu.VMEM((experts, experts * rows), f32),
            dma((STEPS, experts)),
            dma((STEPS, 4)),
            dma((STEPS, 4)),
            dma((STEPS, 4)),
            dma((STEPS, 8)),
            dma((2, 2)),
            dma((2, 2)),
            pltpu.VMEM((experts, 8, 2 * rows), f32),
            pltpu.VMEM((experts, 8, 2 * rows), f32),
            dma((STEPS, 4)),
            dma((STEPS, 4)),
            dma((experts,)),
            dma((experts,)),
            dma((experts,)),
            dma((experts,)),
            dma((experts,)),
            dma((experts,)),
        ],
        compiler_params=pltpu.CompilerParams(
            collective_id=0, has_side_effects=True, vmem_limit_bytes=58 * 1024 * 1024
        ),
    )(
        tokens,
        expert_ids,
        gate_values,
        gate_weight.reshape(gate_weight.shape[1:]),
        up_weight.reshape(up_weight.shape[1:]),
        down_weight.reshape(down_weight.shape[1:]),
        sketch,
        subsets,
    )
    return combined, gram, prune.reshape(-1)


def shards(tokens, expert_ids, gate_values, gate_weight, up_weight, down_weight, sketch, subsets):
    experts = lax.axis_size("expert")
    tok_rows = expert_ids.shape[0]
    top_count = expert_ids.shape[1]
    capacity = min(tok_rows, tok_rows * top_count * 5 // (4 * experts))
    flat_ids = expert_ids.reshape(-1)
    pick_count = flat_ids.shape[0]
    labels = jnp.arange(experts, dtype=jnp.int32)
    member = (flat_ids[:, None] == labels[None, :]).astype(jnp.int32)
    position = jnp.sum((jnp.cumsum(member, axis=0) - 1) * member, axis=1)
    slot_index = flat_ids * capacity + position
    source_row = jnp.arange(pick_count, dtype=jnp.int32) // top_count
    row_table = jnp.zeros((experts * capacity,), jnp.int32).at[slot_index].set(source_row)
    filled = jnp.zeros((experts * capacity,), jnp.bfloat16).at[slot_index].set(1.0)
    whole_rows = lax.all_gather(tokens, "node", axis=1, tiled=True)
    picked = jnp.take(whole_rows, row_table, axis=0) * filled[:, None]
    arrived = lax.all_to_all(
        picked.reshape(experts, capacity, whole_rows.shape[1]),
        "expert",
        split_axis=0,
        concat_axis=0,
        tiled=True,
    )
    model_width = arrived.shape[2]
    slot_rows = arrived.reshape(-1, model_width)
    down_local = down_weight[0]
    sketch_width = sketch.shape[1]
    sketched_down = jnp.dot(
        down_local,
        lax.all_gather(sketch, "node", axis=0, tiled=True),
        preferred_element_type=jnp.float32,
    ).astype(jnp.bfloat16)
    gate_part = jnp.dot(slot_rows, gate_weight[0], preferred_element_type=jnp.float32)
    up_part = jnp.dot(slot_rows, up_weight[0], preferred_element_type=jnp.float32)
    hidden = (jax.nn.silu(gate_part) * up_part).astype(jnp.bfloat16)
    partial_sketch = jnp.dot(hidden, sketched_down, preferred_element_type=jnp.float32)
    returned = lax.all_to_all(
        partial_sketch.reshape(experts, capacity, sketch_width),
        "expert",
        split_axis=0,
        concat_axis=0,
        tiled=True,
    )
    slot_sketch = lax.psum_scatter(returned, "node", scatter_dimension=2, tiled=True).astype(
        jnp.bfloat16
    )
    half_width = slot_sketch.shape[2]
    pick_sketch = jnp.take(slot_sketch.reshape(-1, half_width), slot_index, axis=0)
    pick_sketch = pick_sketch.reshape(tok_rows, top_count, half_width).astype(jnp.float32)
    combined = jnp.einsum("tk,tkc->tc", gate_values, pick_sketch).astype(jnp.bfloat16)
    gated_sketch = gate_values[:, :, None] * pick_sketch
    pair_inner = jnp.einsum("tkc,tlc->tkl", gated_sketch, gated_sketch)
    routing = (expert_ids[:, :, None] == labels[None, None, :]).astype(jnp.float32)
    local_gram = jnp.einsum("tke,tkl,tlf->ef", routing, pair_inner, routing)
    total_gram = lax.psum(local_gram, ("expert", "node"))
    gram_matrix = total_gram / (tok_rows * experts * sketch_width)
    kept_mask = jnp.sum((subsets[:, :, None] == labels[None, None, :]).astype(jnp.float32), axis=1)
    pruned = 1.0 - kept_mask
    prune_error = jnp.einsum("se,ef,sf->s", pruned, gram_matrix, pruned) / jnp.sum(gram_matrix)
    return (combined, gram_matrix, prune_error)


def solution(mesh):
    in_specs = (
        P(("groups", "expert"), "node"),
        P(("groups", "expert"), None),
        P(("groups", "expert"), None),
        P("expert", None, "node"),
        P("expert", None, "node"),
        P("expert", "node", None),
        P("node", None),
        P(),
    )
    out_specs = (P(("groups", "expert"), "node"), P("groups", None), P("groups"))
    plain = mesh.shape["node"] == 1 and mesh.shape["expert"] == 16
    return jax.shard_map(fused if plain else shards, mesh=mesh, in_specs=in_specs, out_specs=out_specs, check_vma=False)
```

```python
import jax
import jax.numpy as jnp
from jax import lax
from jax.experimental import pallas as pl
from jax.experimental.pallas import tpu as pltpu
from jax.sharding import PartitionSpec as P

STEPS = 14
LAG = 1
BOTH = 7
ROW_TILE = 256


def fused_kernel(
    tokens,
    ids,
    gates,
    gate_w,
    up_w,
    down_w,
    sketch,
    subsets,
    combined,
    gram_out,
    prune_out,
    xbuf,
    acc_gate,
    acc_up,
    acc_down,
    sd,
    wbuf,
    dbuf,
    sbuf,
    outbox,
    inbox,
    gated,
    gram_box,
    partial,
    recv_sem,
    up_sem,
    down_sem,
    side_sem,
    core_sem,
    w_sem,
    d_sem,
    slots_out,
    slots_in,
    cross_up,
    cross_down,
    slot_send,
    slot_recv,
    back_send,
    back_recv,
    gram_send,
    gram_recv,
):
    me = lax.axis_index("expert")
    z, y, c = me // 4, (me // 2) % 2, me % 2
    above, below = me + 4, me - 4
    side = z * 4 + (1 - y) * 2 + c
    twin = z * 4 + y * 2 + (1 - c)
    rows, width = tokens.shape
    chunk = width // STEPS
    experts = 16

    def to(device):
        return {"expert": device}

    def weight_loads(k):
        slot = k % 2
        at = pl.ds(pl.multiple_of(k * chunk, chunk), chunk)
        return (
            pltpu.make_async_copy(gate_w.at[at, :], wbuf.at[slot, 0], w_sem.at[slot, 0]),
            pltpu.make_async_copy(up_w.at[at, :], wbuf.at[slot, 1], w_sem.at[slot, 1]),
        )

    def down_loads(k):
        slot = k % 2
        at = pl.ds(pl.multiple_of(k * chunk, chunk), chunk)
        return (
            pltpu.make_async_copy(down_w.at[:, at], dbuf.at[slot], d_sem.at[slot, 0]),
            pltpu.make_async_copy(sketch.at[at, :], sbuf.at[slot], d_sem.at[slot, 1]),
        )

    for load in down_loads(0) + weight_loads(0):
        load.start()

    barrier = pltpu.get_barrier_semaphore()
    for shift in range(1, experts):
        pl.semaphore_signal(
            barrier,
            inc=1,
            device_id=to((me + shift) % experts),
            device_id_type=pl.DeviceIdType.MESH,
        )
    for k in range(STEPS):
        xbuf[k, me] = tokens[:, k * chunk : (k + 1) * chunk]
    acc_gate[...] = jnp.zeros_like(acc_gate)
    acc_up[...] = jnp.zeros_like(acc_up)
    acc_down[...] = jnp.zeros_like(acc_down)

    capacity = outbox.shape[1] // 2
    labels = lax.broadcasted_iota(jnp.int32, (experts, rows), 0)
    member = jnp.zeros((experts, rows), jnp.float32)
    gate_of = jnp.zeros((experts, rows), jnp.float32)
    for j in range(ids.shape[0]):
        named = ids[j : j + 1, :] == labels
        member = member + jnp.where(named, 1.0, 0.0)
        gate_of = gate_of + jnp.where(named, gates[j : j + 1, :], 0.0)
    member = member.astype(jnp.bfloat16)
    first = lax.broadcasted_iota(jnp.int32, (rows, 2 * rows), 0)
    second = lax.broadcasted_iota(jnp.int32, (rows, 2 * rows), 1) % rows

    def turned(mask):
        return lax.dot_general(
            member,
            jnp.where(mask, 1.0, 0.0).astype(jnp.bfloat16),
            (((1,), (0,)), ((), ())),
            preferred_element_type=jnp.float32,
        )

    slots = jnp.where(turned(first == second) > 0.5, turned(first < second), -1.0)
    for e in range(experts):
        slots_out[e] = jnp.broadcast_to(slots[e : e + 1, :], (8, 2 * rows))
    slots_in[me] = slots_out[me]

    def picker(row):
        shape = (2 * capacity, 2 * rows)
        place = lax.broadcasted_iota(jnp.int32, shape, 0)
        half = lax.broadcasted_iota(jnp.int32, shape, 1) >= rows
        late = place >= capacity
        wanted = jnp.where(late, place - capacity, place).astype(jnp.float32)
        wanted = jnp.where(late == half, wanted, -2.0)
        return jnp.where(row == wanted, 1.0, 0.0).astype(jnp.bfloat16)

    pl.semaphore_wait(barrier, experts - 1)

    def send(k, block, sem, target):
        return pltpu.make_async_remote_copy(
            src_ref=xbuf.at[k, block],
            dst_ref=xbuf.at[k, block],
            send_sem=sem,
            recv_sem=recv_sem.at[k, block],
            device_id=to(target),
            device_id_type=pl.DeviceIdType.MESH,
        )

    def slot_copy(block):
        return pltpu.make_async_remote_copy(
            src_ref=slots_out.at[block],
            dst_ref=slots_in.at[me],
            send_sem=slot_send.at[block],
            recv_sem=slot_recv.at[me],
            device_id=to(block),
            device_id_type=pl.DeviceIdType.MESH,
        )

    def slot_arrived(e):
        return pltpu.make_async_remote_copy(
            src_ref=slots_out.at[e],
            dst_ref=slots_in.at[e],
            send_sem=slot_send.at[e],
            recv_sem=slot_recv.at[e],
            device_id=to(twin),
            device_id_type=pl.DeviceIdType.MESH,
        )

    for e in range(experts):

        @pl.when(me != e)
        def _():
            slot_copy(e).start()

    def when_chunk(k, also=None):
        cond = (k >= 0) & (k < STEPS)
        return pl.when(cond if also is None else cond & also)

    def step(s, carry):
        for plane in range(4):
            dist = jnp.abs(z - plane)
            block = plane * 4 + y * 2 + c
            k = s - LAG * dist

            @when_chunk(k)
            def _():
                @pl.when(z != plane)
                def _():
                    send(k, block, up_sem.at[k, plane], twin).wait_recv()

                @pl.when((plane <= z) & (z < 3))
                def _():
                    send(k, block, up_sem.at[k, plane], above).start()

                @pl.when((plane >= z) & (z > 0))
                def _():
                    send(k, block, down_sem.at[k, plane], below).start()

                @pl.when((z == plane) | (k % BOTH != 0))
                def _():
                    send(k, block, side_sem.at[k, plane], side).start()

                send(k, block, core_sem.at[k, plane], twin).start()

        for plane in range(4):
            dist = jnp.abs(z - plane)
            block = plane * 4 + (1 - y) * 2 + c
            k = s - LAG * (dist + 1)

            @when_chunk(k)
            def _():
                send(k, block, core_sem.at[k, 4 + plane], twin).wait_recv()

                @pl.when((plane <= z) & (z < 3) & (k % BOTH == 0))
                def _():
                    send(k, block, cross_up.at[k, plane], above).start()

                @pl.when((plane >= z) & (z > 0) & (k % BOTH == 0))
                def _():
                    send(k, block, cross_down.at[k, plane], below).start()

                send(k, block, core_sem.at[k, 4 + plane], twin).start()

        @pl.when(s < STEPS)
        def _():
            slot = s % 2

            @pl.when(s + 1 < STEPS)
            def _():
                for load in down_loads(s + 1):
                    load.start()

            for load in down_loads(s):
                load.wait()

            @pl.loop(0, down_w.shape[0] // ROW_TILE)
            def _(r):
                at = pl.ds(pl.multiple_of(r * ROW_TILE, ROW_TILE), ROW_TILE)
                acc_down[at, :] += jnp.dot(
                    dbuf[slot, at, :], sbuf[slot], preferred_element_type=jnp.float32
                )

        k = s - 5 * LAG

        @when_chunk(k)
        def _():
            slot = k % 2

            @pl.when(k + 1 < STEPS)
            def _():
                for load in weight_loads(k + 1):
                    load.start()

            for plane in range(4):
                for col in range(2):
                    block = plane * 4 + col * 2 + (1 - c)
                    send(k, block, up_sem.at[k, plane], twin).wait_recv()
            for load in weight_loads(k):
                load.wait()

            @pl.loop(0, experts * rows // ROW_TILE)
            def _(r):
                per = ROW_TILE // rows
                at = pl.ds(pl.multiple_of(r * ROW_TILE, ROW_TILE), ROW_TILE)
                x = xbuf[k, pl.ds(r * per, per)].reshape(ROW_TILE, chunk)
                acc_gate[at, :] += jnp.dot(x, wbuf[slot, 0], preferred_element_type=jnp.float32)
                acc_up[at, :] += jnp.dot(x, wbuf[slot, 1], preferred_element_type=jnp.float32)

        return carry

    lax.fori_loop(0, STEPS + 5 * LAG, step, 0)

    sd[...] = acc_down[...].astype(jnp.bfloat16)

    for e in range(experts):

        @pl.when(me != e)
        def _():
            slot_arrived(e).wait_recv()

    half_width = sd.shape[1] // 2

    def back(block):
        return pltpu.make_async_remote_copy(
            src_ref=outbox.at[block],
            dst_ref=inbox.at[me],
            send_sem=back_send.at[block],
            recv_sem=back_recv.at[me],
            device_id=to(block),
            device_id_type=pl.DeviceIdType.MESH,
        )

    def finish(i, carry):
        plane = (z + 1 + i) % 4
        at = pl.ds(pl.multiple_of(plane * 4 * rows, 4 * rows), 4 * rows)
        g = acc_gate[at, :]
        hidden = (g / (1.0 + jnp.exp(-g)) * acc_up[at, :]).astype(jnp.bfloat16)
        result = jnp.dot(hidden, sd[...], preferred_element_type=jnp.float32).astype(jnp.bfloat16)
        for j in range(4):
            block = plane * 4 + j
            mine = result[j * rows : (j + 1) * rows]
            mine = jnp.concatenate([mine[:, :half_width], mine[:, half_width:]], axis=0)
            outbox[block] = jnp.dot(
                picker(slots_in[block][0:1, :]), mine, preferred_element_type=jnp.float32
            ).astype(jnp.bfloat16)

            @pl.when(block != me)
            def _():
                back(block).start()

        return carry

    lax.fori_loop(0, 4, finish, 0)
    inbox[me] = outbox[me]

    def arrived(e):
        return pltpu.make_async_remote_copy(
            src_ref=outbox.at[e],
            dst_ref=inbox.at[e],
            send_sem=back_send.at[e],
            recv_sem=back_recv.at[e],
            device_id=to(twin),
            device_id_type=pl.DeviceIdType.MESH,
        )

    same_token = lax.broadcasted_iota(jnp.int32, (rows, rows), 0) == lax.broadcasted_iota(
        jnp.int32, (rows, rows), 1
    )
    total = jnp.zeros(combined.shape, jnp.float32)
    for e in range(experts):

        @pl.when(me != e)
        def _():
            arrived(e).wait_recv()

        gate = jnp.sum(jnp.where(same_token, gate_of[e : e + 1, :], 0.0), axis=1, keepdims=True)
        spread = lax.dot_general(
            picker(slots_out[e][0:1, :]),
            inbox[e],
            (((0,), (0,)), ((), ())),
            preferred_element_type=jnp.float32,
        )
        part = gate * jnp.concatenate([spread[:rows], spread[rows:]], axis=1)
        total = total + part
        gated[e * rows : (e + 1) * rows, :] = part.astype(jnp.bfloat16)
    combined[...] = total.astype(combined.dtype)

    flat = experts * rows
    tile = 4 * rows
    row_tok = lax.broadcasted_iota(jnp.int32, (tile, flat), 0) % rows
    col_tok = lax.broadcasted_iota(jnp.int32, (tile, flat), 1) % rows
    same = row_tok == col_tok
    for r in range(4):
        pair = lax.dot_general(
            gated[r * tile : (r + 1) * tile, :],
            gated[...],
            (((1,), (1,)), ((), ())),
            preferred_element_type=jnp.float32,
        )
        pair = jnp.where(same, pair, 0.0).reshape(4, rows, flat)
        partial[r * 4 : (r + 1) * 4, :] = jnp.sum(pair, axis=1)
    owner = lax.broadcasted_iota(jnp.int32, (flat, experts), 0) // rows
    label = lax.broadcasted_iota(jnp.int32, (flat, experts), 1)
    local = jnp.dot(
        partial[...],
        (owner == label).astype(jnp.float32),
        preferred_element_type=jnp.float32,
        precision=lax.Precision.HIGHEST,
    )
    gram_box[me] = local

    def share(shift):
        other = (me + shift) % experts
        return pltpu.make_async_remote_copy(
            src_ref=gram_box.at[me],
            dst_ref=gram_box.at[me],
            send_sem=gram_send.at[shift],
            recv_sem=gram_recv.at[me],
            device_id=to(other),
            device_id_type=pl.DeviceIdType.MESH,
        )

    def shared(e):
        return pltpu.make_async_remote_copy(
            src_ref=gram_box.at[e],
            dst_ref=gram_box.at[e],
            send_sem=gram_send.at[0],
            recv_sem=gram_recv.at[e],
            device_id=to(twin),
            device_id_type=pl.DeviceIdType.MESH,
        )

    for shift in range(1, experts):
        share(shift).start()
    names = subsets[...]
    columns = lax.broadcasted_iota(jnp.int32, (experts, names.shape[1]), 0)
    kept = jnp.zeros((experts, names.shape[1]), jnp.float32)
    for j in range(names.shape[0]):
        kept = kept + jnp.where(names[j : j + 1, :] == columns, 1.0, 0.0)
    pruned = 1.0 - kept

    def collect(k, carry):
        for plane in range(4):
            block = plane * 4 + y * 2 + c
            across = plane * 4 + (1 - y) * 2 + c

            @pl.when((plane <= z) & (z < 3))
            def _():
                send(k, block, up_sem.at[k, plane], above).wait_send()

            @pl.when((plane >= z) & (z > 0))
            def _():
                send(k, block, down_sem.at[k, plane], below).wait_send()

            @pl.when((z == plane) | (k % BOTH != 0))
            def _():
                send(k, block, side_sem.at[k, plane], side).wait_send()

            @pl.when((plane <= z) & (z < 3) & (k % BOTH == 0))
            def _():
                send(k, across, cross_up.at[k, plane], above).wait_send()

            @pl.when((plane >= z) & (z > 0) & (k % BOTH == 0))
            def _():
                send(k, across, cross_down.at[k, plane], below).wait_send()

            send(k, block, core_sem.at[k, plane], twin).wait_send()
            send(k, across, core_sem.at[k, 4 + plane], twin).wait_send()
        return carry

    lax.fori_loop(0, STEPS, collect, 0)
    for e in range(experts):

        @pl.when(me != e)
        def _():
            arrived(e).wait_send()
            slot_arrived(e).wait_send()

    for e in range(experts):

        @pl.when(me != e)
        def _():
            shared(e).wait_recv()

    gram = jnp.sum(gram_box[...], axis=0) / (rows * experts * sketch.shape[1])
    gram_out[...] = gram
    weighed = jnp.dot(
        gram, pruned, preferred_element_type=jnp.float32, precision=lax.Precision.HIGHEST
    )
    prune_out[...] = jnp.sum(weighed * pruned, axis=0, keepdims=True) / jnp.sum(gram)
    for shift in range(1, experts):
        share(shift).wait_send()


def fused(tokens, expert_ids, gate_values, gate_weight, up_weight, down_weight, sketch, subsets):
    rows, width = tokens.shape
    experts = 16
    chunk = width // STEPS
    capacity = min(rows, rows * expert_ids.shape[1] * 5 // (4 * experts))
    hidden_width = gate_weight.shape[2]
    sketch_width = sketch.shape[1]
    bf16, f32 = jnp.bfloat16, jnp.float32
    dma = pltpu.SemaphoreType.DMA
    vmem = pl.BlockSpec(memory_space=pltpu.VMEM)
    hbm = pl.BlockSpec(memory_space=pl.ANY)
    combined, gram, prune = pl.pallas_call(
        fused_kernel,
        out_shape=(
            jax.ShapeDtypeStruct((rows, sketch_width), bf16),
            jax.ShapeDtypeStruct((experts, experts), f32),
            jax.ShapeDtypeStruct((1, subsets.shape[0]), f32),
        ),
        in_specs=[vmem, vmem, vmem, hbm, hbm, hbm, hbm, vmem],
        out_specs=(vmem, vmem, vmem),
        scratch_shapes=[
            pltpu.VMEM((STEPS, experts, rows, chunk), bf16),
            pltpu.VMEM((experts * rows, hidden_width), f32),
            pltpu.VMEM((experts * rows, hidden_width), f32),
            pltpu.VMEM((hidden_width, sketch_width), f32),
            pltpu.VMEM((hidden_width, sketch_width), bf16),
            pltpu.VMEM((2, 2, chunk, hidden_width), bf16),
            pltpu.VMEM((2, hidden_width, chunk), bf16),
            pltpu.VMEM((2, chunk, sketch_width), bf16),
            pltpu.VMEM((experts, 2 * capacity, sketch_width // 2), bf16),
            pltpu.VMEM((experts, 2 * capacity, sketch_width // 2), bf16),
            pltpu.VMEM((experts * rows, sketch_width), bf16),
            pltpu.VMEM((experts, experts, experts), f32),
            pltpu.VMEM((experts, experts * rows), f32),
            dma((STEPS, experts)),
            dma((STEPS, 4)),
            dma((STEPS, 4)),
            dma((STEPS, 4)),
            dma((STEPS, 8)),
            dma((2, 2)),
            dma((2, 2)),
            pltpu.VMEM((experts, 8, 2 * rows), f32),
            pltpu.VMEM((experts, 8, 2 * rows), f32),
            dma((STEPS, 4)),
            dma((STEPS, 4)),
            dma((experts,)),
            dma((experts,)),
            dma((experts,)),
            dma((experts,)),
            dma((experts,)),
            dma((experts,)),
        ],
        compiler_params=pltpu.CompilerParams(
            collective_id=0, has_side_effects=True, vmem_limit_bytes=58 * 1024 * 1024
        ),
    )(
        tokens,
        expert_ids.T,
        gate_values.T,
        gate_weight.reshape(gate_weight.shape[1:]),
        up_weight.reshape(up_weight.shape[1:]),
        down_weight.reshape(down_weight.shape[1:]),
        sketch,
        subsets.T,
    )
    return combined, gram, prune.reshape(-1)


def shards(tokens, expert_ids, gate_values, gate_weight, up_weight, down_weight, sketch, subsets):
    experts = lax.axis_size("expert")
    tok_rows = expert_ids.shape[0]
    top_count = expert_ids.shape[1]
    capacity = min(tok_rows, tok_rows * top_count * 5 // (4 * experts))
    flat_ids = expert_ids.reshape(-1)
    pick_count = flat_ids.shape[0]
    labels = jnp.arange(experts, dtype=jnp.int32)
    member = (flat_ids[:, None] == labels[None, :]).astype(jnp.int32)
    position = jnp.sum((jnp.cumsum(member, axis=0) - 1) * member, axis=1)
    slot_index = flat_ids * capacity + position
    source_row = jnp.arange(pick_count, dtype=jnp.int32) // top_count
    row_table = jnp.zeros((experts * capacity,), jnp.int32).at[slot_index].set(source_row)
    filled = jnp.zeros((experts * capacity,), jnp.bfloat16).at[slot_index].set(1.0)
    whole_rows = lax.all_gather(tokens, "node", axis=1, tiled=True)
    picked = jnp.take(whole_rows, row_table, axis=0) * filled[:, None]
    arrived = lax.all_to_all(
        picked.reshape(experts, capacity, whole_rows.shape[1]),
        "expert",
        split_axis=0,
        concat_axis=0,
        tiled=True,
    )
    model_width = arrived.shape[2]
    slot_rows = arrived.reshape(-1, model_width)
    down_local = down_weight[0]
    sketch_width = sketch.shape[1]
    sketched_down = jnp.dot(
        down_local,
        lax.all_gather(sketch, "node", axis=0, tiled=True),
        preferred_element_type=jnp.float32,
    ).astype(jnp.bfloat16)
    gate_part = jnp.dot(slot_rows, gate_weight[0], preferred_element_type=jnp.float32)
    up_part = jnp.dot(slot_rows, up_weight[0], preferred_element_type=jnp.float32)
    hidden = (jax.nn.silu(gate_part) * up_part).astype(jnp.bfloat16)
    partial_sketch = jnp.dot(hidden, sketched_down, preferred_element_type=jnp.float32)
    returned = lax.all_to_all(
        partial_sketch.reshape(experts, capacity, sketch_width),
        "expert",
        split_axis=0,
        concat_axis=0,
        tiled=True,
    )
    slot_sketch = lax.psum_scatter(returned, "node", scatter_dimension=2, tiled=True).astype(
        jnp.bfloat16
    )
    half_width = slot_sketch.shape[2]
    pick_sketch = jnp.take(slot_sketch.reshape(-1, half_width), slot_index, axis=0)
    pick_sketch = pick_sketch.reshape(tok_rows, top_count, half_width).astype(jnp.float32)
    combined = jnp.einsum("tk,tkc->tc", gate_values, pick_sketch).astype(jnp.bfloat16)
    gated_sketch = gate_values[:, :, None] * pick_sketch
    pair_inner = jnp.einsum("tkc,tlc->tkl", gated_sketch, gated_sketch)
    routing = (expert_ids[:, :, None] == labels[None, None, :]).astype(jnp.float32)
    local_gram = jnp.einsum("tke,tkl,tlf->ef", routing, pair_inner, routing)
    total_gram = lax.psum(local_gram, ("expert", "node"))
    gram_matrix = total_gram / (tok_rows * experts * sketch_width)
    kept_mask = jnp.sum((subsets[:, :, None] == labels[None, None, :]).astype(jnp.float32), axis=1)
    pruned = 1.0 - kept_mask
    prune_error = jnp.einsum("se,ef,sf->s", pruned, gram_matrix, pruned) / jnp.sum(gram_matrix)
    return (combined, gram_matrix, prune_error)


def solution(mesh):
    in_specs = (
        P(("groups", "expert"), "node"),
        P(("groups", "expert"), None),
        P(("groups", "expert"), None),
        P("expert", None, "node"),
        P("expert", None, "node"),
        P("expert", "node", None),
        P("node", None),
        P(),
    )
    out_specs = (P(("groups", "expert"), "node"), P("groups", None), P("groups"))
    plain = mesh.shape["node"] == 1 and mesh.shape["expert"] == 16
    return jax.shard_map(fused if plain else shards, mesh=mesh, in_specs=in_specs, out_specs=out_specs, check_vma=False)
```
